32 devices in a mesh: seq: 4 (over y, core), ctx: 8 (over z, x).
Axes of the slice: x: 2, y: 2, z: 4, core: 2. Of those that a mesh axis runs over, the one named last changes fastest.
Arguments:
- inputs: bfloat16 [24576, 1024], P(('seq', 'ctx')), parts along dimension 0, may hold values from -9 to 9
- qkv_weight: bfloat16 [1024, 3072], replicated, may hold values from -3 to 3
- out_weight: bfloat16 [1024, 1024], replicated, may hold values from -0.1875 to 0.1875
- rand_owner: int32 [384, 3], P(('seq', 'ctx')), parts along dimension 0, may hold values from 0 to 7, all different within a row; in each aligned block of 12 rows (0 to 11, 12 to 23, ...) at most 5 rows name the same one
- rand_local: int32 [384, 3], P(('seq', 'ctx')), parts along dimension 0, may hold values from 0 to 11
Outputs:
- attended: bfloat16 [24576, 1024], P(('seq', 'ctx')), parts along dimension 0
The draws below stay inside these ranges and needn't reach their ends.
There are 4 independent parts, one for each index of `seq`. The reference program is written for one: setup_inputs(seed, part) draws one part's arguments, and reference() takes and returns one part's arrays. A program takes and returns all parts, laid end to end along the dimension named above; an argument that names none is the same for every part. Nothing has to cross between parts.
Inputs may be any that keep to these rules, and one draw needn't show every extreme that they name: `rand_owner`: within the 12 rows of one device no owner is named by more than 5 rows, a bound that some block reaches; the 3 owners of one row differ. Rows of the first and the last block are not used.
All inputs are finite; a program needn't handle non-finite values.
Results may differ from the reference program's by a relative error of at most 0.003.
The reference program's roundings to bfloat16 on the way count: a program that leaves them out, or rounds other values in their place, can miss the bound.
Values may be sent and summed in bfloat16 or wider, within the bound.
A program may use at most 192 MiB of HBM per device.

```python
import math
import jax
import jax.numpy as jnp
import numpy as np
from jax import lax

D = 1024
HEADS = 16
BLOCK = 64
RANDS = 3
TOKENS = 6144
NBLOCKS = 96
BPD = 12
CAP = 5
N_CTX = 8


def draw_inputs(key, part):
    base = jnp.clip(jax.random.normal(key, (TOKENS, D), jnp.float32), -4.5, 4.5)
    direction = jnp.clip(jax.random.normal(jax.random.fold_in(key, 3), (D,), jnp.float32), -3.0, 3.0)
    ramp = jnp.arange(TOKENS, dtype=jnp.float32) * (2.0 / TOKENS) - 1.0
    base = base + ramp[:, None] * direction[None, :]
    return jnp.clip(base, -9.0, 9.0).astype(jnp.bfloat16)


def draw_qkv_weight(key, part):
    base = jnp.clip(jax.random.normal(key, (D, 3 * D), jnp.float32), -5.0, 5.0) / math.sqrt(D)
    return base.astype(jnp.bfloat16)


def touch_ends(values, stream_key, low, top_value):
    longest = values.shape.index(max(values.shape))
    spots = []
    for shift in (0, 1):
        where = [jax.random.randint(jax.random.fold_in(stream_key, axis), (), 0, length) for axis, length in enumerate(values.shape)]
        where[longest] = (where[longest] + shift) % values.shape[longest]
        spots.append(tuple(where))
    return values.at[spots[0]].set(low).at[spots[1]].set(top_value)


def routed_block(stream_key, own, number, rows, number_of, top, limit, slope):
    order = jax.random.permutation(stream_key, number_of)
    crowded, common = portions_of(number_of, rows * top, limit, slope, True), portions_of(number_of, rows * top, limit, slope, False)
    places = jnp.arange(number_of)

    def named(lengths, rotation):
        used = int((lengths > 0).sum())
        fixed = max(1, used // 4)
        passed = fixed + (places - fixed + rotation * (used - fixed)) % max(1, number_of - fixed)
        return jnp.zeros((number_of,), jnp.int32).at[order[jnp.where(places < fixed, places, passed)]].set(jnp.asarray(lengths, jnp.int32))

    lengths = jnp.where(number % 4 == 0, named(crowded, number // 4), named(common, number - number // 4 - 1))
    mixed = jax.random.permutation(jax.random.fold_in(own, 3), number_of)
    donor, taker = mixed[0:number_of // 2 * 2:2], mixed[1:number_of // 2 * 2:2]
    margin = jnp.minimum(lengths[donor] - 1, limit - lengths[taker]) // 2
    margin = jnp.where((donor == order[0]) | (taker == order[0]) | (lengths[taker] == 0), 0, jnp.maximum(margin, 0))
    passed = jax.random.randint(jax.random.fold_in(own, 4), (number_of // 2,), 0, 1 << 20) % (margin + 1)
    lengths = lengths.at[donor].add(-passed).at[taker].add(passed)
    labels = jnp.searchsorted(jnp.cumsum(lengths), jnp.arange(rows * top), side="right").astype(jnp.int32)
    grid = labels.reshape(top, rows).T
    grid = grid[jax.random.permutation(jax.random.fold_in(own, 1), rows)]
    rotation = jax.random.randint(jax.random.fold_in(own, 2), (rows, 1), 0, top)
    return jnp.take_along_axis(grid, (jnp.arange(top)[None, :] + rotation) % top, axis=1)


def portions_of(amount, total, bound, slope, full):
    loads = [(1 << 20) // math.isqrt(grade ** slope) + 1 for grade in range(1, amount + 1)]
    largest = bound if full else min(bound, max(-(-total // amount), total * loads[0] // sum(loads)))
    least = 1 if total - largest >= amount - 1 else 0
    given, rest = [largest] + [least] * (amount - 1), total - largest - least * (amount - 1)
    while rest > 0:
        candidates = [i for i in range(1, amount) if given[i] < largest] or [i for i in range(1, amount) if given[i] < bound]
        whole, budget = sum([loads[i] for i in candidates]), rest
        for i in candidates:
            addition = min(bound - given[i], max(1, budget * loads[i] // whole), rest)
            given[i] = given[i] + addition
            rest = rest - addition
    return np.array(given)


def normal_values(stream_key, shape, scale, most, kind=jnp.bfloat16):
    values = scale * jax.random.normal(stream_key, shape, jnp.float32)
    return jnp.clip(values, min=-most, max=most).astype(kind)


def setup_inputs(seed: int = 0, part: int = 0) -> dict:
    key_list = jax.random.split(jax.random.key(seed), 6)
    own_keys = jax.random.split(jax.random.fold_in(key_list[5], part), 6)
    inputs = draw_inputs(jax.random.fold_in(jax.random.fold_in(key_list[5], part), 71), part)
    qkv_weight = draw_qkv_weight(jax.random.fold_in(key_list[5], 71), part)
    out_weight = normal_values(key_list[2], (D, D), D ** -0.5, 0.1875)
    rand_owner_keys = jax.random.split(jax.random.fold_in(own_keys[3], 1), NBLOCKS // BPD)
    rand_owner_turns = jax.random.permutation(jax.random.fold_in(own_keys[3], 3), NBLOCKS // BPD)
    rand_owner = jax.vmap(lambda own, number: routed_block(jax.random.fold_in(own_keys[3], 2), own, number, BPD, N_CTX, RANDS, CAP, 2))(rand_owner_keys, rand_owner_turns).reshape((NBLOCKS, RANDS))
    rand_local = touch_ends(jax.random.randint(own_keys[4], (NBLOCKS, RANDS), 0, BPD), jax.random.fold_in(own_keys[4], 1), 0, BPD - 1).astype(jnp.int32)
    return dict(inputs=inputs, qkv_weight=qkv_weight, out_weight=out_weight, rand_owner=rand_owner, rand_local=rand_local)


def reference(inputs, qkv_weight, out_weight, rand_owner, rand_local):
    n_rows = inputs.shape[0]
    n_blocks = n_rows // BLOCK
    head_dim = D // HEADS
    inv_root = 1.0 / math.sqrt(head_dim)
    projected = jnp.dot(inputs, qkv_weight, preferred_element_type=jnp.float32).astype(jnp.bfloat16)
    queries = projected[:, :D].reshape(n_rows, HEADS, head_dim)
    keys_all = projected[:, D:2 * D].reshape(n_rows, HEADS, head_dim)
    values_all = projected[:, 2 * D:].reshape(n_rows, HEADS, head_dim)
    glob_queries = jnp.concatenate([queries[:BLOCK], queries[n_rows - BLOCK:]], axis=0).astype(jnp.float32)
    glob_scores = jnp.einsum('qhd,khd->qhk', glob_queries, keys_all.astype(jnp.float32), precision=lax.Precision.HIGHEST) * inv_root
    glob_weights = jax.nn.softmax(glob_scores, axis=-1)
    glob_context = jnp.einsum('qhk,khd->qhd', glob_weights, values_all.astype(jnp.float32), precision=lax.Precision.HIGHEST).reshape(2 * BLOCK, D)
    block_ids = jnp.arange(n_blocks, dtype=jnp.int32)
    rand_ids = (rand_owner * BPD + rand_local).astype(jnp.int32)
    window_ids = jnp.stack([block_ids - 1, block_ids, block_ids + 1], axis=1)
    global_ids = jnp.broadcast_to(jnp.array([0, n_blocks - 1], jnp.int32), (n_blocks, 2))
    fixed_ids = jnp.concatenate([window_ids, global_ids], axis=1)
    window_ok = jnp.stack([block_ids - 1 >= 1, block_ids >= 0, block_ids + 1 < n_blocks - 1], axis=1)
    rand_ok = jnp.all(rand_ids[:, :, None] != fixed_ids[:, None, :], axis=2)
    usable = jnp.concatenate([window_ok, jnp.ones((n_blocks, 2), bool), rand_ok], axis=1)
    all_ids = jnp.clip(jnp.concatenate([fixed_ids, rand_ids], axis=1), 0, n_blocks - 1).astype(jnp.int32)
    key_blocks = keys_all.reshape(n_blocks, BLOCK, HEADS, head_dim)
    value_blocks = values_all.reshape(n_blocks, BLOCK, HEADS, head_dim)
    query_groups = queries.reshape(n_blocks // 8, 8, BLOCK, HEADS, head_dim)

    def attend(packed):
        group_queries, group_ids, group_ok = packed
        group_keys = key_blocks[group_ids].reshape(8, 8 * BLOCK, HEADS, head_dim).astype(jnp.float32)
        group_values = value_blocks[group_ids].reshape(8, 8 * BLOCK, HEADS, head_dim).astype(jnp.float32)
        scores = jnp.einsum('gqhd,gkhd->ghqk', group_queries.astype(jnp.float32), group_keys, precision=lax.Precision.HIGHEST) * inv_root
        live_keys = jnp.repeat(group_ok, BLOCK, axis=1)[:, None, None, :]
        scores = jnp.where(live_keys, scores, -jnp.inf)
        row_top = lax.optimization_barrier(jnp.max(scores, axis=-1, keepdims=True))
        exponent = jnp.exp(scores - row_top)
        weights = (exponent / lax.optimization_barrier(jnp.sum(exponent, axis=-1, keepdims=True))).astype(jnp.bfloat16)
        mixture = jnp.einsum('ghqk,gkhd->gqhd', weights.astype(jnp.float32), group_values, precision=lax.Precision.HIGHEST)
        return mixture.reshape(8 * BLOCK, D)
    context = lax.map(attend, (query_groups, all_ids.reshape(-1, 8, 8), usable.reshape(-1, 8, 8)))
    context = context.reshape(n_rows, D)
    context = jnp.concatenate([glob_context[:BLOCK], context[BLOCK:n_rows - BLOCK], glob_context[BLOCK:]], axis=0).astype(jnp.bfloat16)
    return jnp.dot(context, out_weight, preferred_element_type=jnp.float32).astype(jnp.bfloat16)
```

```python
import functools

import jax
import jax.numpy as jnp
from jax import lax
from jax.experimental import pallas as pl
from jax.experimental.pallas import tpu as pltpu
from jax.sharding import PartitionSpec as P

HEADS = 16
BLOCK = 64
HD = 64
MESH = pl.DeviceIdType.MESH


def request_slots(owners, n_dev, capacity):
    flat_owner = owners.reshape(-1)
    onehot = (flat_owner[:, None] == jnp.arange(n_dev, dtype=jnp.int32)[None, :]).astype(jnp.int32)
    before = jnp.cumsum(onehot, axis=0) - onehot
    rank_of = jnp.sum(before * onehot, axis=1)
    return flat_owner * capacity + rank_of


def greet_all(me, n):
    barrier = pltpu.get_barrier_semaphore()
    for d in range(1, n):
        pl.semaphore_signal(
            barrier, inc=1, device_id={"ctx": lax.rem(me + d, n)}, device_id_type=MESH
        )
    pl.semaphore_wait(barrier, n - 1)


def remote(src, dst, send, recv, target):
    return pltpu.make_async_remote_copy(
        src_ref=src,
        dst_ref=dst,
        send_sem=send,
        recv_sem=recv,
        device_id={"ctx": target},
        device_id_type=MESH,
    )


def rim_kernel(n, rows, x_ref, o_ref, own_sem, edge_sem, send_sem, halo_send, recv_sem):
    me = lax.axis_index("ctx")
    first = x_ref.at[pl.ds(0, BLOCK)]
    last = x_ref.at[pl.ds(rows - BLOCK, BLOCK)]
    prev = o_ref.at[pl.ds(0, BLOCK)]
    after = o_ref.at[pl.ds(rows + BLOCK, BLOCK)]
    glob0 = o_ref.at[pl.ds(rows + 2 * BLOCK, BLOCK)]
    glob1 = o_ref.at[pl.ds(rows + 3 * BLOCK, BLOCK)]
    own = pltpu.make_async_copy(x_ref, o_ref.at[pl.ds(BLOCK, rows)], own_sem)
    own.start()
    greet_all(me, n)
    up, down = lax.rem(me + 1, n), lax.rem(me + n - 1, n)
    to_next = remote(last, prev, halo_send.at[0], recv_sem.at[0], up)
    to_prev = remote(first, after, halo_send.at[1], recv_sem.at[1], down)

    @pl.when(me < n - 1)
    def _():
        to_next.start()

    @pl.when(me > 0)
    def _():
        to_prev.start()

    @pl.when(me == 0)
    def _():
        sends = [remote(first, glob0, send_sem.at[d], recv_sem.at[2], d) for d in range(1, n)]
        for c in sends:
            c.start()
        mine = [
            pltpu.make_async_copy(first, glob0, edge_sem.at[0]),
            pltpu.make_async_copy(first, prev, edge_sem.at[1]),
        ]
        for c in mine:
            c.start()
        for c in mine:
            c.wait()
        for c in sends:
            c.wait_send()

    @pl.when(me == n - 1)
    def _():
        sends = [remote(last, glob1, send_sem.at[d], recv_sem.at[3], d) for d in range(n - 1)]
        for c in sends:
            c.start()
        mine = [
            pltpu.make_async_copy(last, glob1, edge_sem.at[0]),
            pltpu.make_async_copy(last, after, edge_sem.at[1]),
        ]
        for c in mine:
            c.start()
        for c in mine:
            c.wait()
        for c in sends:
            c.wait_send()

    @pl.when(me > 0)
    def _():
        to_prev.wait_send()
        to_next.wait_recv()
        remote(first, glob0, send_sem.at[0], recv_sem.at[2], up).wait_recv()

    @pl.when(me < n - 1)
    def _():
        to_next.wait_send()
        to_prev.wait_recv()
        remote(last, glob1, send_sem.at[0], recv_sem.at[3], up).wait_recv()

    own.wait()


def partial_kernel(rows, width, p_ref, o_ref, lse_ref):
    q_rows = 2 * BLOCK
    row_head = lax.broadcasted_iota(jnp.int32, (2 * q_rows, 128), 0) // q_rows
    col_head = lax.broadcasted_iota(jnp.int32, (2 * q_rows, 128), 1) // HD
    diag = row_head == col_head
    low = lax.broadcasted_iota(jnp.int32, (q_rows, 128), 1) < HD
    for g in range(HEADS // 2):
        c = g * 128
        q = p_ref[pl.ds(rows + 2 * BLOCK, q_rows), pl.ds(c, 128)] * jnp.bfloat16(0.125)
        qd = jnp.where(diag, jnp.concatenate([q, q], axis=0), jnp.zeros_like(q[:1]))
        k = p_ref[pl.ds(BLOCK, rows), pl.ds(width + c, 128)]
        v = p_ref[pl.ds(BLOCK, rows), pl.ds(2 * width + c, 128)]
        s = lax.dot_general(k, qd, (((1,), (1,)), ((), ())), preferred_element_type=jnp.float32)
        m = jnp.max(s, axis=0, keepdims=True)
        e = jnp.exp(s - m)
        total = jnp.sum(e, axis=0, keepdims=True)
        w = e * (1.0 / total)
        hi = w.astype(jnp.bfloat16)
        lo = (w - hi.astype(jnp.float32)).astype(jnp.bfloat16)
        dims = (((0,), (0,)), ((), ()))
        out = lax.dot_general(hi, v, dims, preferred_element_type=jnp.float32)
        out += lax.dot_general(lo, v, dims, preferred_element_type=jnp.float32)
        mixed = jnp.where(low, out[:q_rows], out[q_rows:]).astype(o_ref.dtype)
        o_ref[0, :, pl.ds(c, 128)] = mixed[:BLOCK]
        o_ref[1, :, pl.ds(c, 128)] = mixed[BLOCK:]
        lse_ref[pl.ds(g, 1), :] = m + jnp.log(total)


def collect_kernel(n, part_ref, lse_ref, o_ref, ol_ref, sends, lsends, recvs, lrecvs, locals_):
    me = lax.axis_index("ctx")
    greet_all(me, n)
    for t, target in enumerate((0, n - 1)):
        a = remote(part_ref.at[t], o_ref.at[me], sends.at[t], recvs.at[me], target)
        b = remote(lse_ref, ol_ref.at[me], lsends.at[t], lrecvs.at[me], target)

        @pl.when(me != target)
        def _():
            a.start()
            b.start()

        @pl.when(me == target)
        def _():
            c = pltpu.make_async_copy(part_ref.at[t], o_ref.at[target], locals_.at[0])
            d = pltpu.make_async_copy(lse_ref, ol_ref.at[target], locals_.at[1])
            c.start()
            d.start()
            c.wait()
            d.wait()

    for t, target in enumerate((0, n - 1)):

        @pl.when(me != target)
        def _():
            remote(part_ref.at[t], o_ref.at[me], sends.at[t], recvs.at[me], target).wait_send()
            remote(lse_ref, ol_ref.at[me], lsends.at[t], lrecvs.at[me], target).wait_send()

        @pl.when(me == target)
        def _():
            for src in range(n):
                if src != target:
                    remote(
                        part_ref.at[t], o_ref.at[src], sends.at[t], recvs.at[src], src
                    ).wait_recv()
                    remote(
                        lse_ref, ol_ref.at[src], lsends.at[t], lrecvs.at[src], src
                    ).wait_recv()


def attend_kernel(
    n_local, width, slots, usable, use_glob, p_ref, r0, r1, r2, glob_ref, o_ref
):
    i = pl.program_id(0)
    row_head = lax.broadcasted_iota(jnp.int32, (256, 256), 0) // HD
    col_head = lax.broadcasted_iota(jnp.int32, (256, 256), 1) // HD
    diag = row_head == col_head
    lane_head = lax.broadcasted_iota(jnp.int32, (BLOCK, 256), 1) // HD
    near = pl.ds(pl.multiple_of(i * BLOCK, BLOCK), 3 * BLOCK)
    mine = pl.ds(pl.multiple_of(i * BLOCK + BLOCK, BLOCK), BLOCK)
    ends = pl.ds((n_local + 2) * BLOCK, 2 * BLOCK)
    live = [usable[i * 8 + b] > 0 for b in range(8)]
    for g in range(HEADS // 4):
        c = g * 256
        q = p_ref[mine, pl.ds(c, 256)] * jnp.bfloat16(0.125)
        qd = jnp.where(diag, jnp.concatenate([q] * 4, axis=0), jnp.zeros_like(q[:1]))

        def rows_of(base):
            return jnp.concatenate(
                [p_ref[near, pl.ds((1 + base) * width + c, 256)], p_ref[ends, pl.ds((1 + base) * width + c, 256)]]
                + [r[:, pl.ds(base * width + c, 256)] for r in (r0, r1, r2)],
                axis=0,
            )

        s = lax.dot_general(
            rows_of(0), qd, (((1,), (1,)), ((), ())), preferred_element_type=jnp.float32
        )
        s = jnp.concatenate(
            [
                jnp.where(live[b], s[b * BLOCK : (b + 1) * BLOCK], -jnp.inf)
                if b not in (1, 3, 4)
                else s[b * BLOCK : (b + 1) * BLOCK]
                for b in range(8)
            ],
            axis=0,
        )
        m = jnp.max(s, axis=0, keepdims=True)
        e = jnp.exp(s - m)
        w = (e * (1.0 / jnp.sum(e, axis=0, keepdims=True))).astype(jnp.bfloat16)
        out = lax.dot_general(
            w, rows_of(1), (((0,), (0,)), ((), ())), preferred_element_type=jnp.float32
        )
        ctx = out[:BLOCK]
        for h in range(1, 4):
            ctx = jnp.where(lane_head == h, out[h * BLOCK : (h + 1) * BLOCK], ctx)
        ctx = jnp.where(use_glob[i] > 0, glob_ref[:, pl.ds(c, 256)], ctx)
        o_ref[:, pl.ds(c, 256)] = ctx.astype(o_ref.dtype)


def per_device(inputs, qkv_weight, out_weight, rand_owner, rand_local):
    rows, width = inputs.shape
    n_local = rows // BLOCK
    n = lax.axis_size("ctx")
    me = lax.axis_index("ctx")
    capacity = max(2, (3 * n_local + n - 1) // n)
    any_spec = pl.BlockSpec(memory_space=pl.ANY)
    dma = pltpu.SemaphoreType.DMA

    slot_ids = request_slots(rand_owner, n, capacity)
    table = jnp.zeros((n * capacity,), jnp.int32).at[slot_ids].set(rand_local.reshape(-1))
    asked_for = lax.all_to_all(
        table.reshape(n, capacity), "ctx", split_axis=0, concat_axis=0, tiled=True
    )
    outgoing = inputs.reshape(n_local, BLOCK, width)[asked_for.reshape(-1)]
    outgoing = outgoing.reshape(n, capacity * BLOCK, width)
    arrived = lax.all_to_all(outgoing, "ctx", split_axis=0, concat_axis=0, tiled=True)

    rimmed = pl.pallas_call(
        functools.partial(rim_kernel, n, rows),
        out_shape=jax.ShapeDtypeStruct((rows + 4 * BLOCK, width), inputs.dtype),
        in_specs=[any_spec],
        out_specs=any_spec,
        scratch_shapes=[dma, dma((2,)), dma((n,)), dma((2,)), dma((4,))],
        compiler_params=pltpu.CompilerParams(collective_id=0, has_side_effects=True),
        name="rim",
    )(inputs)
    near = jnp.dot(rimmed, qkv_weight, preferred_element_type=jnp.float32).astype(jnp.bfloat16)

    part, lse = pl.pallas_call(
        functools.partial(partial_kernel, rows, width),
        out_shape=(
            jax.ShapeDtypeStruct((2, BLOCK, width), jnp.bfloat16),
            jax.ShapeDtypeStruct((HEADS // 2, 4 * BLOCK), jnp.float32),
        ),
        compiler_params=pltpu.CompilerParams(vmem_limit_bytes=40 * 1024 * 1024),
        cost_estimate=pl.CostEstimate(flops=10**9, bytes_accessed=7 * 10**6, transcendentals=10**6),
        name="partial",
    )(near)
    parts, lses = pl.pallas_call(
        functools.partial(collect_kernel, n),
        out_shape=(
            jax.ShapeDtypeStruct((n, BLOCK, width), jnp.bfloat16),
            jax.ShapeDtypeStruct((n, HEADS // 2, 4 * BLOCK), jnp.float32),
        ),
        in_specs=[any_spec] * 2,
        out_specs=(any_spec, any_spec),
        scratch_shapes=[dma((2,)), dma((2,)), dma((n,)), dma((n,)), dma((2,))],
        compiler_params=pltpu.CompilerParams(collective_id=1, has_side_effects=True),
        name="collect",
    )(part, lse)
    is_first, is_last = me == 0, me == n - 1
    gather_here = is_first | is_last
    parts = jnp.where(gather_here, parts, 0)
    lses = jnp.where(gather_here, lses, 0.0).reshape(n, HEADS, 2, BLOCK)
    lses = jnp.where(is_first, lses[:, :, 0], lses[:, :, 1])
    share = jax.nn.softmax(lses, axis=0).transpose(0, 2, 1)
    glob = jnp.sum(parts.astype(jnp.float32) * jnp.repeat(share, HD, axis=2), axis=0)

    n_blocks = n_local * n
    block_ids = me * n_local + jnp.arange(n_local, dtype=jnp.int32)
    rand_ids = rand_owner * n_local + rand_local
    window_ids = jnp.stack([block_ids - 1, block_ids, block_ids + 1], axis=1)
    global_ids = jnp.broadcast_to(jnp.array([0, n_blocks - 1], jnp.int32), (n_local, 2))
    fixed_ids = jnp.concatenate([window_ids, global_ids], axis=1)
    window_ok = jnp.stack(
        [block_ids - 1 >= 1, block_ids >= 0, block_ids + 1 < n_blocks - 1], axis=1
    )
    rand_ok = jnp.all(rand_ids[:, :, None] != fixed_ids[:, None, :], axis=2)
    usable = jnp.concatenate([window_ok, jnp.ones((n_local, 2), bool), rand_ok], axis=1)
    use_glob = ((block_ids == 0) | (block_ids == n_blocks - 1)).astype(jnp.int32)

    far = jnp.dot(
        arrived.reshape(n * capacity * BLOCK, width),
        qkv_weight[:, width:],
        preferred_element_type=jnp.float32,
    ).astype(jnp.bfloat16)

    def pick(s):
        return pl.BlockSpec((BLOCK, 2 * width), lambda i, slots, *_: (slots[i * 3 + s], 0))

    context = pl.pallas_call(
        functools.partial(attend_kernel, n_local, width),
        out_shape=jax.ShapeDtypeStruct((rows, width), jnp.bfloat16),
        grid_spec=pltpu.PrefetchScalarGridSpec(
            num_scalar_prefetch=3,
            grid=(n_local,),
            in_specs=[
                pl.BlockSpec((rows + 4 * BLOCK, 3 * width), lambda i, *_: (0, 0)),
                pick(0),
                pick(1),
                pick(2),
                pl.BlockSpec((BLOCK, width), lambda i, *_: (0, 0)),
            ],
            out_specs=pl.BlockSpec((BLOCK, width), lambda i, *_: (i, 0)),
        ),
        compiler_params=pltpu.CompilerParams(vmem_limit_bytes=40 * 1024 * 1024),
        name="attend",
    )(
        slot_ids,
        usable.astype(jnp.int32).reshape(-1),
        use_glob,
        near,
        far,
        far,
        far,
        glob,
    )
    return jnp.dot(context, out_weight, preferred_element_type=jnp.float32).astype(jnp.bfloat16)


def solution(mesh):
    in_specs = (P(("seq", "ctx"), None), P(), P(), P(("seq", "ctx"), None), P(("seq", "ctx"), None))
    out_specs = P(("seq", "ctx"), None)
    return jax.shard_map(
        per_device, mesh=mesh, in_specs=in_specs, out_specs=out_specs, check_vma=False
    )
```

```python
import functools

import jax
import jax.numpy as jnp
from jax import lax
from jax.experimental import pallas as pl
from jax.experimental.pallas import tpu as pltpu
from jax.sharding import PartitionSpec as P

HEADS = 16
BLOCK = 64
HD = 64
MESH = pl.DeviceIdType.MESH


def request_slots(owners, n_dev, capacity):
    flat_owner = owners.reshape(-1)
    onehot = (flat_owner[:, None] == jnp.arange(n_dev, dtype=jnp.int32)[None, :]).astype(jnp.int32)
    before = jnp.cumsum(onehot, axis=0) - onehot
    rank_of = jnp.sum(before * onehot, axis=1)
    return flat_owner * capacity + rank_of


def greet_all(me, n):
    barrier = pltpu.get_barrier_semaphore()
    for d in range(1, n):
        pl.semaphore_signal(
            barrier, inc=1, device_id={"ctx": lax.rem(me + d, n)}, device_id_type=MESH
        )
    pl.semaphore_wait(barrier, n - 1)


def remote(src, dst, send, recv, target):
    return pltpu.make_async_remote_copy(
        src_ref=src,
        dst_ref=dst,
        send_sem=send,
        recv_sem=recv,
        device_id={"ctx": target},
        device_id_type=MESH,
    )


def rim_kernel(
    n, rows, x_ref, t_ref, o_ref, a_ref, own_sem, edge_sem, send_sem, halo_send, recv_sem, asks, asked
):
    me = lax.axis_index("ctx")
    first = x_ref.at[pl.ds(0, BLOCK)]
    last = x_ref.at[pl.ds(rows - BLOCK, BLOCK)]
    prev = o_ref.at[pl.ds(0, BLOCK)]
    after = o_ref.at[pl.ds(rows + BLOCK, BLOCK)]
    glob0 = o_ref.at[pl.ds(rows + 2 * BLOCK, BLOCK)]
    glob1 = o_ref.at[pl.ds(rows + 3 * BLOCK, BLOCK)]
    own = pltpu.make_async_copy(x_ref, o_ref.at[pl.ds(BLOCK, rows)], own_sem)
    own.start()
    keep = pltpu.make_async_copy(t_ref.at[me], a_ref.at[me], asks.at[0])
    keep.start()
    greet_all(me, n)
    requests = []
    for d in range(1, n):
        to = lax.rem(me + d, n)
        requests.append(remote(t_ref.at[to], a_ref.at[me], asks.at[d], asked.at[d], to))
        requests[-1].start()
    up, down = lax.rem(me + 1, n), lax.rem(me + n - 1, n)
    to_next = remote(last, prev, halo_send.at[0], recv_sem.at[0], up)
    to_prev = remote(first, after, halo_send.at[1], recv_sem.at[1], down)

    @pl.when(me < n - 1)
    def _():
        to_next.start()

    @pl.when(me > 0)
    def _():
        to_prev.start()

    @pl.when(me == 0)
    def _():
        sends = [remote(first, glob0, send_sem.at[d], recv_sem.at[2], d) for d in range(1, n)]
        for c in sends:
            c.start()
        mine = [
            pltpu.make_async_copy(first, glob0, edge_sem.at[0]),
            pltpu.make_async_copy(first, prev, edge_sem.at[1]),
        ]
        for c in mine:
            c.start()
        for c in mine:
            c.wait()
        for c in sends:
            c.wait_send()

    @pl.when(me == n - 1)
    def _():
        sends = [remote(last, glob1, send_sem.at[d], recv_sem.at[3], d) for d in range(n - 1)]
        for c in sends:
            c.start()
        mine = [
            pltpu.make_async_copy(last, glob1, edge_sem.at[0]),
            pltpu.make_async_copy(last, after, edge_sem.at[1]),
        ]
        for c in mine:
            c.start()
        for c in mine:
            c.wait()
        for c in sends:
            c.wait_send()

    @pl.when(me > 0)
    def _():
        to_prev.wait_send()
        to_next.wait_recv()
        remote(first, glob0, send_sem.at[0], recv_sem.at[2], up).wait_recv()

    @pl.when(me < n - 1)
    def _():
        to_next.wait_send()
        to_prev.wait_recv()
        remote(last, glob1, send_sem.at[0], recv_sem.at[3], up).wait_recv()

    for d in range(1, n):
        requests[d - 1].wait_send()
        source = lax.rem(me + n - d, n)
        remote(t_ref.at[source], a_ref.at[source], asks.at[d], asked.at[d], source).wait_recv()
    keep.wait()
    own.wait()


def partial_kernel(rows, width, p_ref, o_ref, lse_ref):
    q_rows = 2 * BLOCK
    row_head = lax.broadcasted_iota(jnp.int32, (2 * q_rows, 128), 0) // q_rows
    col_head = lax.broadcasted_iota(jnp.int32, (2 * q_rows, 128), 1) // HD
    diag = row_head == col_head
    low = lax.broadcasted_iota(jnp.int32, (q_rows, 128), 1) < HD
    for g in range(HEADS // 2):
        c = g * 128
        q = p_ref[pl.ds(rows + 2 * BLOCK, q_rows), pl.ds(c, 128)] * jnp.bfloat16(0.125)
        qd = jnp.where(diag, jnp.concatenate([q, q], axis=0), jnp.zeros_like(q[:1]))
        k = p_ref[pl.ds(BLOCK, rows), pl.ds(width + c, 128)]
        v = p_ref[pl.ds(BLOCK, rows), pl.ds(2 * width + c, 128)]
        s = lax.dot_general(k, qd, (((1,), (1,)), ((), ())), preferred_element_type=jnp.float32)
        m = jnp.max(s, axis=0, keepdims=True)
        e = jnp.exp(s - m)
        total = jnp.sum(e, axis=0, keepdims=True)
        w = e * (1.0 / total)
        hi = w.astype(jnp.bfloat16)
        lo = (w - hi.astype(jnp.float32)).astype(jnp.bfloat16)
        dims = (((0,), (0,)), ((), ()))
        out = lax.dot_general(hi, v, dims, preferred_element_type=jnp.float32)
        out += lax.dot_general(lo, v, dims, preferred_element_type=jnp.float32)
        mixed = jnp.where(low, out[:q_rows], out[q_rows:]).astype(o_ref.dtype)
        o_ref[0, :, pl.ds(c, 128)] = mixed[:BLOCK]
        o_ref[1, :, pl.ds(c, 128)] = mixed[BLOCK:]
        lse_ref[pl.ds(g, 1), :] = m + jnp.log(total)


def collect_kernel(n, part_ref, lse_ref, o_ref, ol_ref, sends, lsends, recvs, lrecvs, locals_):
    me = lax.axis_index("ctx")
    greet_all(me, n)
    for t, target in enumerate((0, n - 1)):
        a = remote(part_ref.at[t], o_ref.at[me], sends.at[t], recvs.at[me], target)
        b = remote(lse_ref, ol_ref.at[me], lsends.at[t], lrecvs.at[me], target)

        @pl.when(me != target)
        def _():
            a.start()
            b.start()

        @pl.when(me == target)
        def _():
            c = pltpu.make_async_copy(part_ref.at[t], o_ref.at[target], locals_.at[0])
            d = pltpu.make_async_copy(lse_ref, ol_ref.at[target], locals_.at[1])
            c.start()
            d.start()
            c.wait()
            d.wait()

    for t, target in enumerate((0, n - 1)):

        @pl.when(me != target)
        def _():
            remote(part_ref.at[t], o_ref.at[me], sends.at[t], recvs.at[me], target).wait_send()
            remote(lse_ref, ol_ref.at[me], lsends.at[t], lrecvs.at[me], target).wait_send()

        @pl.when(me == target)
        def _():
            for src in range(n):
                if src != target:
                    remote(
                        part_ref.at[t], o_ref.at[src], sends.at[t], recvs.at[src], src
                    ).wait_recv()
                    remote(
                        lse_ref, ol_ref.at[src], lsends.at[t], lrecvs.at[src], src
                    ).wait_recv()


def attend_kernel(
    n_local, width, sa, sb, late, usable, use_glob, p_ref, a0, a1, a2, b0, b1, b2, glob_ref, o_ref
):
    i = pl.program_id(0)
    row_head = lax.broadcasted_iota(jnp.int32, (256, 256), 0) // HD
    col_head = lax.broadcasted_iota(jnp.int32, (256, 256), 1) // HD
    diag = row_head == col_head
    lane_head = lax.broadcasted_iota(jnp.int32, (BLOCK, 256), 1) // HD
    near = pl.ds(pl.multiple_of(i * BLOCK, BLOCK), 3 * BLOCK)
    mine = pl.ds(pl.multiple_of(i * BLOCK + BLOCK, BLOCK), BLOCK)
    ends = pl.ds((n_local + 2) * BLOCK, 2 * BLOCK)
    is_late = [late[i * 3 + s] > 0 for s in range(3)]
    live = [usable[i * 8 + b] > 0 for b in range(8)]
    for g in range(HEADS // 4):
        c = g * 256
        q = p_ref[mine, pl.ds(c, 256)] * jnp.bfloat16(0.125)
        qd = jnp.where(diag, jnp.concatenate([q] * 4, axis=0), jnp.zeros_like(q[:1]))

        def rows_of(base):
            return jnp.concatenate(
                [p_ref[near, pl.ds((1 + base) * width + c, 256)], p_ref[ends, pl.ds((1 + base) * width + c, 256)]]
                + [
                    jnp.where(w, b[:, pl.ds(base * width + c, 256)], a[:, pl.ds(base * width + c, 256)])
                    for w, a, b in zip(is_late, (a0, a1, a2), (b0, b1, b2))
                ],
                axis=0,
            )

        s = lax.dot_general(
            rows_of(0), qd, (((1,), (1,)), ((), ())), preferred_element_type=jnp.float32
        )
        s = jnp.concatenate(
            [
                jnp.where(live[b], s[b * BLOCK : (b + 1) * BLOCK], -jnp.inf)
                if b not in (1, 3, 4)
                else s[b * BLOCK : (b + 1) * BLOCK]
                for b in range(8)
            ],
            axis=0,
        )
        m = jnp.max(s, axis=0, keepdims=True)
        e = jnp.exp(s - m)
        w = (e * (1.0 / jnp.sum(e, axis=0, keepdims=True))).astype(jnp.bfloat16)
        out = lax.dot_general(
            w, rows_of(1), (((0,), (0,)), ((), ())), preferred_element_type=jnp.float32
        )
        ctx = out[:BLOCK]
        for h in range(1, 4):
            ctx = jnp.where(lane_head == h, out[h * BLOCK : (h + 1) * BLOCK], ctx)
        ctx = jnp.where(use_glob[i] > 0, glob_ref[:, pl.ds(c, 256)], ctx)
        o_ref[:, pl.ds(c, 256)] = ctx.astype(o_ref.dtype)


def per_device(inputs, qkv_weight, out_weight, rand_owner, rand_local):
    rows, width = inputs.shape
    n_local = rows // BLOCK
    n = lax.axis_size("ctx")
    me = lax.axis_index("ctx")
    capacity = max(2, (3 * n_local + n - 1) // n)
    any_spec = pl.BlockSpec(memory_space=pl.ANY)
    dma = pltpu.SemaphoreType.DMA

    slot_ids = request_slots(rand_owner, n, capacity)
    table = jnp.zeros((n * capacity,), jnp.int32).at[slot_ids].set(rand_local.reshape(-1))
    table = jnp.pad(table.reshape(n, 1, capacity), ((0, 0), (0, 7), (0, 128 - capacity)))

    rimmed, asked_for = pl.pallas_call(
        functools.partial(rim_kernel, n, rows),
        out_shape=(
            jax.ShapeDtypeStruct((rows + 4 * BLOCK, width), inputs.dtype),
            jax.ShapeDtypeStruct(table.shape, table.dtype),
        ),
        in_specs=[any_spec] * 2,
        out_specs=(any_spec, any_spec),
        scratch_shapes=[dma, dma((2,)), dma((n,)), dma((2,)), dma((4,)), dma((n,)), dma((n,))],
        compiler_params=pltpu.CompilerParams(collective_id=0, has_side_effects=True),
        name="rim",
    )(inputs, table)
    asked_for = asked_for[:, 0, :capacity]
    head = capacity - 1
    blocks = inputs.reshape(n_local, BLOCK, width)

    def sent(picked):
        return blocks[picked.reshape(-1)].reshape(n, -1, width)

    def exchange(outgoing):
        return lax.all_to_all(outgoing, "ctx", split_axis=0, concat_axis=0, tiled=True)

    outgoing_b = sent(asked_for[:, head:])
    arrived_a = exchange(sent(asked_for[:, :head]))
    near = jnp.dot(rimmed, qkv_weight, preferred_element_type=jnp.float32).astype(jnp.bfloat16)

    part, lse = pl.pallas_call(
        functools.partial(partial_kernel, rows, width),
        out_shape=(
            jax.ShapeDtypeStruct((2, BLOCK, width), jnp.bfloat16),
            jax.ShapeDtypeStruct((HEADS // 2, 4 * BLOCK), jnp.float32),
        ),
        compiler_params=pltpu.CompilerParams(vmem_limit_bytes=40 * 1024 * 1024),
        cost_estimate=pl.CostEstimate(flops=10**9, bytes_accessed=7 * 10**6, transcendentals=10**6),
        name="partial",
    )(near)
    parts, lses = pl.pallas_call(
        functools.partial(collect_kernel, n),
        out_shape=(
            jax.ShapeDtypeStruct((n, BLOCK, width), jnp.bfloat16),
            jax.ShapeDtypeStruct((n, HEADS // 2, 4 * BLOCK), jnp.float32),
        ),
        in_specs=[any_spec] * 2,
        out_specs=(any_spec, any_spec),
        scratch_shapes=[dma((2,)), dma((2,)), dma((n,)), dma((n,)), dma((2,))],
        compiler_params=pltpu.CompilerParams(collective_id=1, has_side_effects=True),
        name="collect",
    )(part, lse)
    outgoing_b, parts = lax.optimization_barrier((outgoing_b, parts))
    arrived_b = exchange(outgoing_b)
    is_first, is_last = me == 0, me == n - 1
    gather_here = is_first | is_last
    parts = jnp.where(gather_here, parts, 0)
    lses = jnp.where(gather_here, lses, 0.0).reshape(n, HEADS, 2, BLOCK)
    lses = jnp.where(is_first, lses[:, :, 0], lses[:, :, 1])
    share = jax.nn.softmax(lses, axis=0).transpose(0, 2, 1)
    glob = jnp.sum(parts.astype(jnp.float32) * jnp.repeat(share, HD, axis=2), axis=0)

    n_blocks = n_local * n
    block_ids = me * n_local + jnp.arange(n_local, dtype=jnp.int32)
    rand_ids = rand_owner * n_local + rand_local
    window_ids = jnp.stack([block_ids - 1, block_ids, block_ids + 1], axis=1)
    global_ids = jnp.broadcast_to(jnp.array([0, n_blocks - 1], jnp.int32), (n_local, 2))
    fixed_ids = jnp.concatenate([window_ids, global_ids], axis=1)
    window_ok = jnp.stack(
        [block_ids - 1 >= 1, block_ids >= 0, block_ids + 1 < n_blocks - 1], axis=1
    )
    rand_ok = jnp.all(rand_ids[:, :, None] != fixed_ids[:, None, :], axis=2)
    usable = jnp.concatenate([window_ok, jnp.ones((n_local, 2), bool), rand_ok], axis=1)
    use_glob = ((block_ids == 0) | (block_ids == n_blocks - 1)).astype(jnp.int32)

    kv_weight = qkv_weight[:, width:]

    def project(rows_in):
        return jnp.dot(
            rows_in.reshape(-1, width), kv_weight, preferred_element_type=jnp.float32
        ).astype(jnp.bfloat16)

    far_a, far_b = project(arrived_a), project(arrived_b)
    owner, rank = slot_ids // capacity, slot_ids % capacity
    late = (rank == head).astype(jnp.int32)
    slots_a = jnp.where(late > 0, 0, owner * head + rank)
    slots_b = jnp.where(late > 0, owner, 0)

    def pick(s, which):
        return pl.BlockSpec(
            (BLOCK, 2 * width), lambda i, *refs: (refs[which][i * 3 + s], 0)
        )

    context = pl.pallas_call(
        functools.partial(attend_kernel, n_local, width),
        out_shape=jax.ShapeDtypeStruct((rows, width), jnp.bfloat16),
        grid_spec=pltpu.PrefetchScalarGridSpec(
            num_scalar_prefetch=5,
            grid=(n_local,),
            in_specs=[
                pl.BlockSpec((rows + 4 * BLOCK, 3 * width), lambda i, *_: (0, 0)),
                pick(0, 0),
                pick(1, 0),
                pick(2, 0),
                pick(0, 1),
                pick(1, 1),
                pick(2, 1),
                pl.BlockSpec((BLOCK, width), lambda i, *_: (0, 0)),
            ],
            out_specs=pl.BlockSpec((BLOCK, width), lambda i, *_: (i, 0)),
        ),
        compiler_params=pltpu.CompilerParams(vmem_limit_bytes=40 * 1024 * 1024),
        name="attend",
    )(
        slots_a,
        slots_b,
        late,
        usable.astype(jnp.int32).reshape(-1),
        use_glob,
        near,
        far_a,
        far_a,
        far_a,
        far_b,
        far_b,
        far_b,
        glob,
    )
    return jnp.dot(context, out_weight, preferred_element_type=jnp.float32).astype(jnp.bfloat16)


def solution(mesh):
    in_specs = (P(("seq", "ctx"), None), P(), P(), P(("seq", "ctx"), None), P(("seq", "ctx"), None))
    out_specs = P(("seq", "ctx"), None)
    return jax.shard_map(
        per_device, mesh=mesh, in_specs=in_specs, out_specs=out_specs, check_vma=False
    )
```

```python
import functools

import jax
import jax.numpy as jnp
from jax import lax
from jax.experimental import pallas as pl
from jax.experimental.pallas import tpu as pltpu
from jax.sharding import PartitionSpec as P

HEADS = 16
BLOCK = 64
HD = 64
MESH = pl.DeviceIdType.MESH


def request_slots(owners, n_dev, capacity):
    flat_owner = owners.reshape(-1)
    onehot = (flat_owner[:, None] == jnp.arange(n_dev, dtype=jnp.int32)[None, :]).astype(jnp.int32)
    before = jnp.cumsum(onehot, axis=0) - onehot
    rank_of = jnp.sum(before * onehot, axis=1)
    return flat_owner * capacity + rank_of


def greet_all(me, n):
    barrier = pltpu.get_barrier_semaphore()
    for d in range(1, n):
        pl.semaphore_signal(
            barrier, inc=1, device_id={"ctx": lax.rem(me + d, n)}, device_id_type=MESH
        )
    pl.semaphore_wait(barrier, n - 1)


def remote(src, dst, send, recv, target):
    return pltpu.make_async_remote_copy(
        src_ref=src,
        dst_ref=dst,
        send_sem=send,
        recv_sem=recv,
        device_id={"ctx": target},
        device_id_type=MESH,
    )


def rim_kernel(
    n, rows, x_ref, t_ref, o_ref, a_ref, edge_sem, send_sem, halo_send, recv_sem, asks, asked
):
    me = lax.axis_index("ctx")
    first = x_ref.at[pl.ds(0, BLOCK)]
    last = x_ref.at[pl.ds(rows - BLOCK, BLOCK)]
    prev, after, glob0, glob1 = (o_ref.at[pl.ds(b * BLOCK, BLOCK)] for b in range(4))
    keep = pltpu.make_async_copy(t_ref.at[me], a_ref.at[me], asks.at[0])
    keep.start()
    greet_all(me, n)
    requests = []
    for d in range(1, n):
        to = lax.rem(me + d, n)
        requests.append(remote(t_ref.at[to], a_ref.at[me], asks.at[d], asked.at[d], to))
        requests[-1].start()
    up, down = lax.rem(me + 1, n), lax.rem(me + n - 1, n)
    to_next = remote(last, prev, halo_send.at[0], recv_sem.at[0], up)
    to_prev = remote(first, after, halo_send.at[1], recv_sem.at[1], down)

    @pl.when(me < n - 1)
    def _():
        to_next.start()

    @pl.when(me > 0)
    def _():
        to_prev.start()

    @pl.when(me == 0)
    def _():
        sends = [remote(first, glob0, send_sem.at[d], recv_sem.at[2], d) for d in range(1, n)]
        for c in sends:
            c.start()
        mine = [
            pltpu.make_async_copy(first, glob0, edge_sem.at[0]),
            pltpu.make_async_copy(first, prev, edge_sem.at[1]),
        ]
        for c in mine:
            c.start()
        for c in mine:
            c.wait()
        for c in sends:
            c.wait_send()

    @pl.when(me == n - 1)
    def _():
        sends = [remote(last, glob1, send_sem.at[d], recv_sem.at[3], d) for d in range(n - 1)]
        for c in sends:
            c.start()
        mine = [
            pltpu.make_async_copy(last, glob1, edge_sem.at[0]),
            pltpu.make_async_copy(last, after, edge_sem.at[1]),
        ]
        for c in mine:
            c.start()
        for c in mine:
            c.wait()
        for c in sends:
            c.wait_send()

    @pl.when(me > 0)
    def _():
        to_prev.wait_send()
        to_next.wait_recv()
        remote(first, glob0, send_sem.at[0], recv_sem.at[2], up).wait_recv()

    @pl.when(me < n - 1)
    def _():
        to_next.wait_send()
        to_prev.wait_recv()
        remote(last, glob1, send_sem.at[0], recv_sem.at[3], up).wait_recv()

    for d in range(1, n):
        requests[d - 1].wait_send()
        source = lax.rem(me + n - d, n)
        remote(t_ref.at[source], a_ref.at[source], asks.at[d], asked.at[d], source).wait_recv()
    keep.wait()


def partial_kernel(rows, width, p_ref, o_ref, lse_ref):
    q_rows = 2 * BLOCK
    row_head = lax.broadcasted_iota(jnp.int32, (2 * q_rows, 128), 0) // q_rows
    col_head = lax.broadcasted_iota(jnp.int32, (2 * q_rows, 128), 1) // HD
    diag = row_head == col_head
    low = lax.broadcasted_iota(jnp.int32, (q_rows, 128), 1) < HD
    for g in range(HEADS // 2):
        c = g * 128
        q = p_ref[pl.ds(rows + 2 * BLOCK, q_rows), pl.ds(c, 128)] * jnp.bfloat16(0.125)
        qd = jnp.where(diag, jnp.concatenate([q, q], axis=0), jnp.zeros_like(q[:1]))
        k = p_ref[pl.ds(BLOCK, rows), pl.ds(width + c, 128)]
        v = p_ref[pl.ds(BLOCK, rows), pl.ds(2 * width + c, 128)]
        s = lax.dot_general(k, qd, (((1,), (1,)), ((), ())), preferred_element_type=jnp.float32)
        m = jnp.max(s, axis=0, keepdims=True)
        e = jnp.exp(s - m)
        total = jnp.sum(e, axis=0, keepdims=True)
        w = e * (1.0 / total)
        hi = w.astype(jnp.bfloat16)
        lo = (w - hi.astype(jnp.float32)).astype(jnp.bfloat16)
        dims = (((0,), (0,)), ((), ()))
        out = lax.dot_general(hi, v, dims, preferred_element_type=jnp.float32)
        out += lax.dot_general(lo, v, dims, preferred_element_type=jnp.float32)
        mixed = jnp.where(low, out[:q_rows], out[q_rows:]).astype(o_ref.dtype)
        o_ref[0, :, pl.ds(c, 128)] = mixed[:BLOCK]
        o_ref[1, :, pl.ds(c, 128)] = mixed[BLOCK:]
        lse_ref[pl.ds(g, 1), :] = m + jnp.log(total)


def collect_kernel(n, part_ref, lse_ref, o_ref, ol_ref, sends, lsends, recvs, lrecvs, locals_):
    me = lax.axis_index("ctx")
    greet_all(me, n)
    for t, target in enumerate((0, n - 1)):
        a = remote(part_ref.at[t], o_ref.at[me], sends.at[t], recvs.at[me], target)
        b = remote(lse_ref, ol_ref.at[me], lsends.at[t], lrecvs.at[me], target)

        @pl.when(me != target)
        def _():
            a.start()
            b.start()

        @pl.when(me == target)
        def _():
            c = pltpu.make_async_copy(part_ref.at[t], o_ref.at[target], locals_.at[0])
            d = pltpu.make_async_copy(lse_ref, ol_ref.at[target], locals_.at[1])
            c.start()
            d.start()
            c.wait()
            d.wait()

    for t, target in enumerate((0, n - 1)):

        @pl.when(me != target)
        def _():
            remote(part_ref.at[t], o_ref.at[me], sends.at[t], recvs.at[me], target).wait_send()
            remote(lse_ref, ol_ref.at[me], lsends.at[t], lrecvs.at[me], target).wait_send()

        @pl.when(me == target)
        def _():
            for src in range(n):
                if src != target:
                    remote(
                        part_ref.at[t], o_ref.at[src], sends.at[t], recvs.at[src], src
                    ).wait_recv()
                    remote(
                        lse_ref, ol_ref.at[src], lsends.at[t], lrecvs.at[src], src
                    ).wait_recv()


def attend_kernel(
    n_local, width, slots, usable, use_glob, p_ref, r0, r1, r2, glob_ref, o_ref
):
    i = pl.program_id(0)
    row_head = lax.broadcasted_iota(jnp.int32, (256, 256), 0) // HD
    col_head = lax.broadcasted_iota(jnp.int32, (256, 256), 1) // HD
    diag = row_head == col_head
    lane_head = lax.broadcasted_iota(jnp.int32, (BLOCK, 256), 1) // HD
    near = pl.ds(pl.multiple_of(i * BLOCK, BLOCK), 3 * BLOCK)
    mine = pl.ds(pl.multiple_of(i * BLOCK + BLOCK, BLOCK), BLOCK)
    ends = pl.ds((n_local + 2) * BLOCK, 2 * BLOCK)
    live = [usable[i * 8 + b] > 0 for b in range(8)]
    for g in range(HEADS // 4):
        c = g * 256
        q = p_ref[mine, pl.ds(c, 256)] * jnp.bfloat16(0.125)
        qd = jnp.where(diag, jnp.concatenate([q] * 4, axis=0), jnp.zeros_like(q[:1]))

        def rows_of(base):
            return jnp.concatenate(
                [p_ref[near, pl.ds((1 + base) * width + c, 256)], p_ref[ends, pl.ds((1 + base) * width + c, 256)]]
                + [r[:, pl.ds(base * width + c, 256)] for r in (r0, r1, r2)],
                axis=0,
            )

        s = lax.dot_general(
            rows_of(0), qd, (((1,), (1,)), ((), ())), preferred_element_type=jnp.float32
        )
        s = jnp.concatenate(
            [
                jnp.where(live[b], s[b * BLOCK : (b + 1) * BLOCK], -jnp.inf)
                if b not in (1, 3, 4)
                else s[b * BLOCK : (b + 1) * BLOCK]
                for b in range(8)
            ],
            axis=0,
        )
        m = jnp.max(s, axis=0, keepdims=True)
        e = jnp.exp(s - m)
        w = (e * (1.0 / jnp.sum(e, axis=0, keepdims=True))).astype(jnp.bfloat16)
        out = lax.dot_general(
            w, rows_of(1), (((0,), (0,)), ((), ())), preferred_element_type=jnp.float32
        )
        ctx = out[:BLOCK]
        for h in range(1, 4):
            ctx = jnp.where(lane_head == h, out[h * BLOCK : (h + 1) * BLOCK], ctx)
        ctx = jnp.where(use_glob[i] > 0, glob_ref[:, pl.ds(c, 256)], ctx)
        o_ref[:, pl.ds(c, 256)] = ctx.astype(o_ref.dtype)


def per_device(inputs, qkv_weight, out_weight, rand_owner, rand_local):
    rows, width = inputs.shape
    n_local = rows // BLOCK
    n = lax.axis_size("ctx")
    me = lax.axis_index("ctx")
    capacity = max(2, (3 * n_local + n - 1) // n)
    any_spec = pl.BlockSpec(memory_space=pl.ANY)
    dma = pltpu.SemaphoreType.DMA

    slot_ids = request_slots(rand_owner, n, capacity)
    table = jnp.zeros((n * capacity,), jnp.int32).at[slot_ids].set(rand_local.reshape(-1))
    table = jnp.pad(table.reshape(n, 1, capacity), ((0, 0), (0, 7), (0, 128 - capacity)))

    edges, asked_for = pl.pallas_call(
        functools.partial(rim_kernel, n, rows),
        out_shape=(
            jax.ShapeDtypeStruct((4 * BLOCK, width), inputs.dtype),
            jax.ShapeDtypeStruct(table.shape, table.dtype),
        ),
        in_specs=[any_spec] * 2,
        out_specs=(any_spec, any_spec),
        scratch_shapes=[dma((2,)), dma((n,)), dma((2,)), dma((4,)), dma((n,)), dma((n,))],
        compiler_params=pltpu.CompilerParams(collective_id=0, has_side_effects=True),
        name="rim",
    )(inputs, table)
    asked_for = asked_for[:, 0, :capacity]
    outgoing = inputs.reshape(n_local, BLOCK, width)[asked_for.reshape(-1)]
    outgoing = outgoing.reshape(n, capacity * BLOCK, width)
    outgoing, edges = lax.optimization_barrier((outgoing, edges))
    arrived = lax.all_to_all(outgoing, "ctx", split_axis=0, concat_axis=0, tiled=True)
    rimmed = jnp.concatenate([edges[:BLOCK], inputs, edges[BLOCK:]], axis=0)
    near = jnp.dot(rimmed, qkv_weight, preferred_element_type=jnp.float32).astype(jnp.bfloat16)

    part, lse = pl.pallas_call(
        functools.partial(partial_kernel, rows, width),
        out_shape=(
            jax.ShapeDtypeStruct((2, BLOCK, width), jnp.bfloat16),
            jax.ShapeDtypeStruct((HEADS // 2, 4 * BLOCK), jnp.float32),
        ),
        compiler_params=pltpu.CompilerParams(vmem_limit_bytes=40 * 1024 * 1024),
        cost_estimate=pl.CostEstimate(flops=10**9, bytes_accessed=7 * 10**6, transcendentals=10**6),
        name="partial",
    )(near)
    parts, lses = pl.pallas_call(
        functools.partial(collect_kernel, n),
        out_shape=(
            jax.ShapeDtypeStruct((n, BLOCK, width), jnp.bfloat16),
            jax.ShapeDtypeStruct((n, HEADS // 2, 4 * BLOCK), jnp.float32),
        ),
        in_specs=[any_spec] * 2,
        out_specs=(any_spec, any_spec),
        scratch_shapes=[dma((2,)), dma((2,)), dma((n,)), dma((n,)), dma((2,))],
        compiler_params=pltpu.CompilerParams(collective_id=1, has_side_effects=True),
        name="collect",
    )(part, lse)
    is_first, is_last = me == 0, me == n - 1
    gather_here = is_first | is_last
    parts = jnp.where(gather_here, parts, 0)
    lses = jnp.where(gather_here, lses, 0.0).reshape(n, HEADS, 2, BLOCK)
    lses = jnp.where(is_first, lses[:, :, 0], lses[:, :, 1])
    share = jax.nn.softmax(lses, axis=0).transpose(0, 2, 1)
    glob = jnp.sum(parts.astype(jnp.float32) * jnp.repeat(share, HD, axis=2), axis=0)

    n_blocks = n_local * n
    block_ids = me * n_local + jnp.arange(n_local, dtype=jnp.int32)
    rand_ids = rand_owner * n_local + rand_local
    window_ids = jnp.stack([block_ids - 1, block_ids, block_ids + 1], axis=1)
    global_ids = jnp.broadcast_to(jnp.array([0, n_blocks - 1], jnp.int32), (n_local, 2))
    fixed_ids = jnp.concatenate([window_ids, global_ids], axis=1)
    window_ok = jnp.stack(
        [block_ids - 1 >= 1, block_ids >= 0, block_ids + 1 < n_blocks - 1], axis=1
    )
    rand_ok = jnp.all(rand_ids[:, :, None] != fixed_ids[:, None, :], axis=2)
    usable = jnp.concatenate([window_ok, jnp.ones((n_local, 2), bool), rand_ok], axis=1)
    use_glob = ((block_ids == 0) | (block_ids == n_blocks - 1)).astype(jnp.int32)

    far = jnp.dot(
        arrived.reshape(n * capacity * BLOCK, width),
        qkv_weight[:, width:],
        preferred_element_type=jnp.float32,
    ).astype(jnp.bfloat16)

    def pick(s):
        return pl.BlockSpec((BLOCK, 2 * width), lambda i, slots, *_: (slots[i * 3 + s], 0))

    context = pl.pallas_call(
        functools.partial(attend_kernel, n_local, width),
        out_shape=jax.ShapeDtypeStruct((rows, width), jnp.bfloat16),
        grid_spec=pltpu.PrefetchScalarGridSpec(
            num_scalar_prefetch=3,
            grid=(n_local,),
            in_specs=[
                pl.BlockSpec((rows + 4 * BLOCK, 3 * width), lambda i, *_: (0, 0)),
                pick(0),
                pick(1),
                pick(2),
                pl.BlockSpec((BLOCK, width), lambda i, *_: (0, 0)),
            ],
            out_specs=pl.BlockSpec((BLOCK, width), lambda i, *_: (i, 0)),
        ),
        compiler_params=pltpu.CompilerParams(vmem_limit_bytes=40 * 1024 * 1024),
        name="attend",
    )(
        slot_ids,
        usable.astype(jnp.int32).reshape(-1),
        use_glob,
        near,
        far,
        far,
        far,
        glob,
    )
    return jnp.dot(context, out_weight, preferred_element_type=jnp.float32).astype(jnp.bfloat16)


def solution(mesh):
    in_specs = (P(("seq", "ctx"), None), P(), P(), P(("seq", "ctx"), None), P(("seq", "ctx"), None))
    out_specs = P(("seq", "ctx"), None)
    return jax.shard_map(
        per_device, mesh=mesh, in_specs=in_specs, out_specs=out_specs, check_vma=False
    )
```

```python
import functools

import jax
import jax.numpy as jnp
from jax import lax
from jax.experimental import pallas as pl
from jax.experimental.pallas import tpu as pltpu
from jax.sharding import PartitionSpec as P

HEADS = 16
BLOCK = 64
HD = 64
MESH = pl.DeviceIdType.MESH


def request_slots(owners, n_dev, capacity):
    flat_owner = owners.reshape(-1)
    onehot = (flat_owner[:, None] == jnp.arange(n_dev, dtype=jnp.int32)[None, :]).astype(jnp.int32)
    before = jnp.cumsum(onehot, axis=0) - onehot
    rank_of = jnp.sum(before * onehot, axis=1)
    return flat_owner * capacity + rank_of


def greet_all(me, n):
    barrier = pltpu.get_barrier_semaphore()
    for d in range(1, n):
        pl.semaphore_signal(
            barrier, inc=1, device_id={"ctx": lax.rem(me + d, n)}, device_id_type=MESH
        )
    pl.semaphore_wait(barrier, n - 1)


def remote(src, dst, send, recv, target):
    return pltpu.make_async_remote_copy(
        src_ref=src,
        dst_ref=dst,
        send_sem=send,
        recv_sem=recv,
        device_id={"ctx": target},
        device_id_type=MESH,
    )


def rim_kernel(
    n, rows, x_ref, t_ref, o_ref, a_ref, edge_sem, send_sem, halo_send, recv_sem, asks, asked
):
    me = lax.axis_index("ctx")
    first = x_ref.at[pl.ds(0, BLOCK)]
    last = x_ref.at[pl.ds(rows - BLOCK, BLOCK)]
    prev, after, glob0, glob1 = (o_ref.at[pl.ds(b * BLOCK, BLOCK)] for b in range(4))
    keep = pltpu.make_async_copy(t_ref.at[me], a_ref.at[me], asks.at[0])
    keep.start()
    greet_all(me, n)
    requests = []
    for d in range(1, n):
        to = lax.rem(me + d, n)
        requests.append(remote(t_ref.at[to], a_ref.at[me], asks.at[d], asked.at[d], to))
        requests[-1].start()
    up, down = lax.rem(me + 1, n), lax.rem(me + n - 1, n)
    to_next = remote(last, prev, halo_send.at[0], recv_sem.at[0], up)
    to_prev = remote(first, after, halo_send.at[1], recv_sem.at[1], down)

    @pl.when(me < n - 1)
    def _():
        to_next.start()

    @pl.when(me > 0)
    def _():
        to_prev.start()

    @pl.when(me == 0)
    def _():
        sends = [remote(first, glob0, send_sem.at[d], recv_sem.at[2], d) for d in range(1, n)]
        for c in sends:
            c.start()
        mine = [
            pltpu.make_async_copy(first, glob0, edge_sem.at[0]),
            pltpu.make_async_copy(first, prev, edge_sem.at[1]),
        ]
        for c in mine:
            c.start()
        for c in mine:
            c.wait()
        for c in sends:
            c.wait_send()

    @pl.when(me == n - 1)
    def _():
        sends = [remote(last, glob1, send_sem.at[d], recv_sem.at[3], d) for d in range(n - 1)]
        for c in sends:
            c.start()
        mine = [
            pltpu.make_async_copy(last, glob1, edge_sem.at[0]),
            pltpu.make_async_copy(last, after, edge_sem.at[1]),
        ]
        for c in mine:
            c.start()
        for c in mine:
            c.wait()
        for c in sends:
            c.wait_send()

    @pl.when(me > 0)
    def _():
        to_prev.wait_send()
        to_next.wait_recv()
        remote(first, glob0, send_sem.at[0], recv_sem.at[2], up).wait_recv()

    @pl.when(me < n - 1)
    def _():
        to_next.wait_send()
        to_prev.wait_recv()
        remote(last, glob1, send_sem.at[0], recv_sem.at[3], up).wait_recv()

    for d in range(1, n):
        requests[d - 1].wait_send()
        source = lax.rem(me + n - d, n)
        remote(t_ref.at[source], a_ref.at[source], asks.at[d], asked.at[d], source).wait_recv()
    keep.wait()


def partial_kernel(rows, width, p_ref, o_ref, lse_ref):
    q_rows = 2 * BLOCK
    row_head = lax.broadcasted_iota(jnp.int32, (2 * q_rows, 128), 0) // q_rows
    col_head = lax.broadcasted_iota(jnp.int32, (2 * q_rows, 128), 1) // HD
    diag = row_head == col_head
    low = lax.broadcasted_iota(jnp.int32, (q_rows, 128), 1) < HD
    for g in range(HEADS // 2):
        c = g * 128
        q = p_ref[pl.ds(rows + 2 * BLOCK, q_rows), pl.ds(c, 128)] * jnp.bfloat16(0.125)
        qd = jnp.where(diag, jnp.concatenate([q, q], axis=0), jnp.zeros_like(q[:1]))
        k = p_ref[pl.ds(BLOCK, rows), pl.ds(width + c, 128)]
        v = p_ref[pl.ds(BLOCK, rows), pl.ds(2 * width + c, 128)]
        s = lax.dot_general(k, qd, (((1,), (1,)), ((), ())), preferred_element_type=jnp.float32)
        m = jnp.max(s, axis=0, keepdims=True)
        e = jnp.exp(s - m)
        total = jnp.sum(e, axis=0, keepdims=True)
        w = e * (1.0 / total)
        hi = w.astype(jnp.bfloat16)
        lo = (w - hi.astype(jnp.float32)).astype(jnp.bfloat16)
        dims = (((0,), (0,)), ((), ()))
        out = lax.dot_general(hi, v, dims, preferred_element_type=jnp.float32)
        out += lax.dot_general(lo, v, dims, preferred_element_type=jnp.float32)
        mixed = jnp.where(low, out[:q_rows], out[q_rows:]).astype(o_ref.dtype)
        o_ref[0, :, pl.ds(c, 128)] = mixed[:BLOCK]
        o_ref[1, :, pl.ds(c, 128)] = mixed[BLOCK:]
        lse_ref[pl.ds(g, 1), :] = m + jnp.log(total)


def collect_kernel(n, part_ref, lse_ref, o_ref, ol_ref, sends, lsends, recvs, lrecvs, locals_):
    me = lax.axis_index("ctx")
    greet_all(me, n)
    for t, target in enumerate((0, n - 1)):
        a = remote(part_ref.at[t], o_ref.at[me], sends.at[t], recvs.at[me], target)
        b = remote(lse_ref, ol_ref.at[me], lsends.at[t], lrecvs.at[me], target)

        @pl.when(me != target)
        def _():
            a.start()
            b.start()

        @pl.when(me == target)
        def _():
            c = pltpu.make_async_copy(part_ref.at[t], o_ref.at[target], locals_.at[0])
            d = pltpu.make_async_copy(lse_ref, ol_ref.at[target], locals_.at[1])
            c.start()
            d.start()
            c.wait()
            d.wait()

    for t, target in enumerate((0, n - 1)):

        @pl.when(me != target)
        def _():
            remote(part_ref.at[t], o_ref.at[me], sends.at[t], recvs.at[me], target).wait_send()
            remote(lse_ref, ol_ref.at[me], lsends.at[t], lrecvs.at[me], target).wait_send()

        @pl.when(me == target)
        def _():
            for src in range(n):
                if src != target:
                    remote(
                        part_ref.at[t], o_ref.at[src], sends.at[t], recvs.at[src], src
                    ).wait_recv()
                    remote(
                        lse_ref, ol_ref.at[src], lsends.at[t], lrecvs.at[src], src
                    ).wait_recv()


def attend_kernel(
    n_local, width, sa, sb, late, usable, use_glob, p_ref, a0, a1, a2, b0, b1, b2, glob_ref, o_ref
):
    i = pl.program_id(0)
    row_head = lax.broadcasted_iota(jnp.int32, (256, 256), 0) // HD
    col_head = lax.broadcasted_iota(jnp.int32, (256, 256), 1) // HD
    diag = row_head == col_head
    lane_head = lax.broadcasted_iota(jnp.int32, (BLOCK, 256), 1) // HD
    near = pl.ds(pl.multiple_of(i * BLOCK, BLOCK), 3 * BLOCK)
    mine = pl.ds(pl.multiple_of(i * BLOCK + BLOCK, BLOCK), BLOCK)
    ends = pl.ds((n_local + 2) * BLOCK, 2 * BLOCK)
    is_late = [late[i * 3 + s] > 0 for s in range(3)]
    live = [usable[i * 8 + b] > 0 for b in range(8)]
    for g in range(HEADS // 4):
        c = g * 256
        q = p_ref[mine, pl.ds(c, 256)] * jnp.bfloat16(0.125)
        qd = jnp.where(diag, jnp.concatenate([q] * 4, axis=0), jnp.zeros_like(q[:1]))

        def rows_of(base):
            return jnp.concatenate(
                [p_ref[near, pl.ds((1 + base) * width + c, 256)], p_ref[ends, pl.ds((1 + base) * width + c, 256)]]
                + [
                    jnp.where(w, b[:, pl.ds(base * width + c, 256)], a[:, pl.ds(base * width + c, 256)])
                    for w, a, b in zip(is_late, (a0, a1, a2), (b0, b1, b2))
                ],
                axis=0,
            )

        s = lax.dot_general(
            rows_of(0), qd, (((1,), (1,)), ((), ())), preferred_element_type=jnp.float32
        )
        s = jnp.concatenate(
            [
                jnp.where(live[b], s[b * BLOCK : (b + 1) * BLOCK], -jnp.inf)
                if b not in (1, 3, 4)
                else s[b * BLOCK : (b + 1) * BLOCK]
                for b in range(8)
            ],
            axis=0,
        )
        m = jnp.max(s, axis=0, keepdims=True)
        e = jnp.exp(s - m)
        w = (e * (1.0 / jnp.sum(e, axis=0, keepdims=True))).astype(jnp.bfloat16)
        out = lax.dot_general(
            w, rows_of(1), (((0,), (0,)), ((), ())), preferred_element_type=jnp.float32
        )
        ctx = out[:BLOCK]
        for h in range(1, 4):
            ctx = jnp.where(lane_head == h, out[h * BLOCK : (h + 1) * BLOCK], ctx)
        ctx = jnp.where(use_glob[i] > 0, glob_ref[:, pl.ds(c, 256)], ctx)
        o_ref[:, pl.ds(c, 256)] = ctx.astype(o_ref.dtype)


def per_device(inputs, qkv_weight, out_weight, rand_owner, rand_local):
    rows, width = inputs.shape
    n_local = rows // BLOCK
    n = lax.axis_size("ctx")
    me = lax.axis_index("ctx")
    capacity = max(2, (3 * n_local + n - 1) // n)
    any_spec = pl.BlockSpec(memory_space=pl.ANY)
    dma = pltpu.SemaphoreType.DMA

    slot_ids = request_slots(rand_owner, n, capacity)
    table = jnp.zeros((n * capacity,), jnp.int32).at[slot_ids].set(rand_local.reshape(-1))
    table = jnp.pad(table.reshape(n, 1, capacity), ((0, 0), (0, 7), (0, 128 - capacity)))

    edges, asked_for = pl.pallas_call(
        functools.partial(rim_kernel, n, rows),
        out_shape=(
            jax.ShapeDtypeStruct((4 * BLOCK, width), inputs.dtype),
            jax.ShapeDtypeStruct(table.shape, table.dtype),
        ),
        in_specs=[any_spec] * 2,
        out_specs=(any_spec, any_spec),
        scratch_shapes=[dma((2,)), dma((n,)), dma((2,)), dma((4,)), dma((n,)), dma((n,))],
        compiler_params=pltpu.CompilerParams(collective_id=0, has_side_effects=True),
        name="rim",
    )(inputs, table)
    asked_for = asked_for[:, 0, :capacity]
    head = capacity - 1
    blocks = inputs.reshape(n_local, BLOCK, width)

    def sent(picked):
        return blocks[picked.reshape(-1)].reshape(n, -1, width)

    def exchange(outgoing):
        return lax.all_to_all(outgoing, "ctx", split_axis=0, concat_axis=0, tiled=True)

    outgoing_a, outgoing_b, edges = lax.optimization_barrier(
        (sent(asked_for[:, :head]), sent(asked_for[:, head:]), edges)
    )
    arrived_a = exchange(outgoing_a)
    rimmed = jnp.concatenate([edges[:BLOCK], inputs, edges[BLOCK:]], axis=0)
    near = jnp.dot(rimmed, qkv_weight, preferred_element_type=jnp.float32).astype(jnp.bfloat16)

    part, lse = pl.pallas_call(
        functools.partial(partial_kernel, rows, width),
        out_shape=(
            jax.ShapeDtypeStruct((2, BLOCK, width), jnp.bfloat16),
            jax.ShapeDtypeStruct((HEADS // 2, 4 * BLOCK), jnp.float32),
        ),
        compiler_params=pltpu.CompilerParams(vmem_limit_bytes=40 * 1024 * 1024),
        cost_estimate=pl.CostEstimate(flops=10**9, bytes_accessed=7 * 10**6, transcendentals=10**6),
        name="partial",
    )(near)
    parts, lses = pl.pallas_call(
        functools.partial(collect_kernel, n),
        out_shape=(
            jax.ShapeDtypeStruct((n, BLOCK, width), jnp.bfloat16),
            jax.ShapeDtypeStruct((n, HEADS // 2, 4 * BLOCK), jnp.float32),
        ),
        in_specs=[any_spec] * 2,
        out_specs=(any_spec, any_spec),
        scratch_shapes=[dma((2,)), dma((2,)), dma((n,)), dma((n,)), dma((2,))],
        compiler_params=pltpu.CompilerParams(collective_id=1, has_side_effects=True),
        name="collect",
    )(part, lse)
    outgoing_b, arrived_a, parts = lax.optimization_barrier((outgoing_b, arrived_a, parts))
    arrived_b = exchange(outgoing_b)
    is_first, is_last = me == 0, me == n - 1
    gather_here = is_first | is_last
    parts = jnp.where(gather_here, parts, 0)
    lses = jnp.where(gather_here, lses, 0.0).reshape(n, HEADS, 2, BLOCK)
    lses = jnp.where(is_first, lses[:, :, 0], lses[:, :, 1])
    share = jax.nn.softmax(lses, axis=0).transpose(0, 2, 1)
    glob = jnp.sum(parts.astype(jnp.float32) * jnp.repeat(share, HD, axis=2), axis=0)

    n_blocks = n_local * n
    block_ids = me * n_local + jnp.arange(n_local, dtype=jnp.int32)
    rand_ids = rand_owner * n_local + rand_local
    window_ids = jnp.stack([block_ids - 1, block_ids, block_ids + 1], axis=1)
    global_ids = jnp.broadcast_to(jnp.array([0, n_blocks - 1], jnp.int32), (n_local, 2))
    fixed_ids = jnp.concatenate([window_ids, global_ids], axis=1)
    window_ok = jnp.stack(
        [block_ids - 1 >= 1, block_ids >= 0, block_ids + 1 < n_blocks - 1], axis=1
    )
    rand_ok = jnp.all(rand_ids[:, :, None] != fixed_ids[:, None, :], axis=2)
    usable = jnp.concatenate([window_ok, jnp.ones((n_local, 2), bool), rand_ok], axis=1)
    use_glob = ((block_ids == 0) | (block_ids == n_blocks - 1)).astype(jnp.int32)

    kv_weight = qkv_weight[:, width:]

    def project(rows_in):
        return jnp.dot(
            rows_in.reshape(-1, width), kv_weight, preferred_element_type=jnp.float32
        ).astype(jnp.bfloat16)

    far_a, far_b = project(arrived_a), project(arrived_b)
    owner, rank = slot_ids // capacity, slot_ids % capacity
    late = (rank == head).astype(jnp.int32)
    slots_a = jnp.where(late > 0, 0, owner * head + rank)
    slots_b = jnp.where(late > 0, owner, 0)

    def pick(s, which):
        return pl.BlockSpec(
            (BLOCK, 2 * width), lambda i, *refs: (refs[which][i * 3 + s], 0)
        )

    context = pl.pallas_call(
        functools.partial(attend_kernel, n_local, width),
        out_shape=jax.ShapeDtypeStruct((rows, width), jnp.bfloat16),
        grid_spec=pltpu.PrefetchScalarGridSpec(
            num_scalar_prefetch=5,
            grid=(n_local,),
            in_specs=[
                pl.BlockSpec((rows + 4 * BLOCK, 3 * width), lambda i, *_: (0, 0)),
                pick(0, 0),
                pick(1, 0),
                pick(2, 0),
                pick(0, 1),
                pick(1, 1),
                pick(2, 1),
                pl.BlockSpec((BLOCK, width), lambda i, *_: (0, 0)),
            ],
            out_specs=pl.BlockSpec((BLOCK, width), lambda i, *_: (i, 0)),
        ),
        compiler_params=pltpu.CompilerParams(vmem_limit_bytes=40 * 1024 * 1024),
        name="attend",
    )(
        slots_a,
        slots_b,
        late,
        usable.astype(jnp.int32).reshape(-1),
        use_glob,
        near,
        far_a,
        far_a,
        far_a,
        far_b,
        far_b,
        far_b,
        glob,
    )
    return jnp.dot(context, out_weight, preferred_element_type=jnp.float32).astype(jnp.bfloat16)


def solution(mesh):
    in_specs = (P(("seq", "ctx"), None), P(), P(), P(("seq", "ctx"), None), P(("seq", "ctx"), None))
    out_specs = P(("seq", "ctx"), None)
    return jax.shard_map(
        per_device, mesh=mesh, in_specs=in_specs, out_specs=out_specs, check_vma=False
    )
```
